32 devices in a mesh: tm: 4 (over z), space: 8 (over y, x, core).
Axes of the slice: x: 2, y: 2, z: 4, core: 2. Of those that a mesh axis runs over, the one named last changes fastest.
Arguments:
- snaps: bfloat16 [4096, 3, 16384], P('tm', None, 'space')
- phase_bin: int32 [4096], P('tm'), may hold values from 0 to 15, as said below
- owner_order: int32 [16], replicated, may hold values from 0 to 15, each once
- modes: bfloat16 [16, 128, 3, 16384], P(None, None, None, 'space'), may hold values from -0.02734375 to 0.02734375
Outputs:
- phase_mean: bfloat16 [16, 3, 16384], P('tm', None, 'space')
- coefficients: float32 [4096, 128], P('tm')
The draws below stay inside these ranges and needn't reach their ends.
Inputs may be any that keep to these rules, and one draw needn't show every extreme that they name: `phase_bin`: every bin is named by at least one snapshot; in each aligned block of 1024 snapshots no bin is named more than 128 times.
All inputs are finite; a program needn't handle non-finite values.
Results may differ from the reference program's by a relative error of at most 0.0068.
Values may be sent and summed in bfloat16 or wider, within the bound.
A program may use at most 192 MiB of HBM per device.

```python
import jax
import jax.numpy as jnp
from jax import lax

NBINS = 16
MODES = 128
COMP = 3
T_DEV = 1024
T_SNAP = 4096
CELLS = 16384


def bins_helper(key):
    steps = jnp.arange(T_SNAP, dtype=jnp.int32)
    local = steps % T_DEV
    block = steps // T_DEV
    start = jax.random.randint(jax.random.fold_in(key, 21), (), 0, NBINS).astype(jnp.int32)
    heavy = (start + block) % NBINS
    cls = local // 2 % NBINS
    jitter = jax.random.randint(jax.random.fold_in(key, 11), (T_SNAP,), 0, 3).astype(jnp.int32)
    jitter = jnp.where(cls == heavy, 0, jitter)
    jitter = jnp.where(cls == (heavy + NBINS - 1) % NBINS, 1, jitter)
    jitter = jnp.where(cls == (heavy + NBINS - 2) % NBINS, 2, jitter)
    return (local // 2 + jitter * (local % 2)) % NBINS


def draw_phase_bin(key, part):
    return bins_helper(key)


def draw_snaps(key, part):
    bins_now = bins_helper(key)
    pattern = jax.random.normal(jax.random.fold_in(key, 12), (NBINS, COMP, CELLS), jnp.float32)
    noise = jax.random.normal(jax.random.fold_in(key, 13), (T_SNAP, COMP, CELLS), jnp.float32)
    return (2.0 * pattern[bins_now] + noise).astype(jnp.bfloat16)


def level_of(stream_key, extent, split, low, high):
    loudness = 1.0
    for axis_at, parts in split:
        heights = jax.random.uniform(jax.random.fold_in(jax.random.fold_in(stream_key, 6), axis_at), (parts,), jnp.float32, low / len(split), high / len(split))
        loudness = loudness * jnp.repeat(jnp.exp(heights), extent[axis_at] // parts).reshape((-1,) + (1,) * (len(extent) - 1 - axis_at))
    return loudness


def centred(stream_key, extent, deviation, limit, split=(), kind=jnp.bfloat16):
    drawn = jax.random.normal(stream_key, extent, jnp.float32) * deviation
    if len(split) > 0:
        drawn = level_of(stream_key, extent, split, -0.22, 0.18) * drawn
    return jnp.clip(drawn, min=-limit, max=limit).astype(kind)


def setup_inputs(seed: int = 0) -> dict:
    splits = jax.random.split(jax.random.key(seed), 5)
    snaps = draw_snaps(jax.random.fold_in(splits[4], 71), 0)
    phase_bin = draw_phase_bin(jax.random.fold_in(splits[4], 71), 0)
    owner_order = jax.random.permutation(splits[2], NBINS).astype(jnp.int32)
    modes = centred(splits[3], (NBINS, MODES, COMP, CELLS), (COMP * CELLS) ** -0.5, 0.02734375, ((3, 8),))
    return {"snaps": snaps, "phase_bin": phase_bin, "owner_order": owner_order, "modes": modes}


def reference(snaps, phase_bin, owner_order, modes):
    flattened = snaps.reshape(T_SNAP, COMP * CELLS)
    bin_ids = jnp.arange(NBINS, dtype=jnp.int32)
    onehot = (phase_bin[None, :] == bin_ids[:, None])
    bin_sum = jnp.dot(onehot.astype(jnp.bfloat16), flattened, preferred_element_type=jnp.float32)
    bin_count = jnp.sum(onehot.astype(jnp.float32), axis=1)
    bin_mean = (bin_sum / bin_count[:, None]).astype(jnp.bfloat16)
    phase_mean = bin_mean[owner_order].reshape(NBINS, COMP, CELLS)
    fluct = (flattened.astype(jnp.float32) - bin_mean[phase_bin].astype(jnp.float32)).astype(jnp.bfloat16)
    modes_flat = modes.reshape(NBINS, MODES, COMP * CELLS)
    fluct_blocks = fluct.reshape(T_SNAP // 8, 8, COMP * CELLS)
    bin_blocks = phase_bin.reshape(T_SNAP // 8, 8)

    def one_block(pair):
        block_rows, block_bins = pair
        chosen = modes_flat[block_bins].astype(jnp.float32)
        return jnp.einsum("tk,tmk->tm", block_rows.astype(jnp.float32), chosen)

    coefficients = lax.map(one_block, (fluct_blocks, bin_blocks)).reshape(T_SNAP, MODES)
    return phase_mean, coefficients
```

```python
import functools

import jax
import jax.numpy as jnp
from jax import lax
from jax.experimental import pallas as pl
from jax.experimental.pallas import tpu as pltpu
from jax.sharding import PartitionSpec as P

MESH = pl.DeviceIdType.MESH
F32 = jnp.float32
BF16 = jnp.bfloat16
NT = (((1,), (1,)), ((), ()))


def kernel(
    tm, space, binrow, binb, ownb, snaps, modes, coef_out, mean_out,
    X, mo, acc, sums, cnt, rsum, rcnt, mean, sendc, rsc, agc, mj,
    xsem, msem, s_sum, r_sum, s_cnt, r_cnt, s_mean, r_mean, s_rs, r_rs, s_ag, r_ag,
):
    comp, rows, cells = X.shape
    bins = modes.shape[0]
    nm = modes.shape[2]
    w = cells // tm
    blk = rows // space
    chunk = 256
    me_t = lax.axis_index("tm")
    me_s = lax.axis_index("space")

    xcopies = [pltpu.make_async_copy(snaps.at[c], X.at[c], xsem.at[c]) for c in range(comp)]
    for cp in xcopies:
        cp.start()
    for b in range(bins):
        pltpu.make_async_copy(modes.at[b], mo.at[:, pl.ds(b * nm, nm), :], msem.at[b]).start()

    barrier = pltpu.get_barrier_semaphore()
    for d in range(1, tm):
        pl.semaphore_signal(barrier, inc=1, device_id={"tm": lax.rem(me_t + d, tm)}, device_id_type=MESH)
    for d in range(1, space):
        pl.semaphore_signal(barrier, inc=1, device_id={"space": lax.rem(me_s + d, space)}, device_id_type=MESH)
    pl.semaphore_wait(barrier, tm - 1 + space - 1)

    hit = ownb[:, 0:1] == binrow[...]
    onehot = jnp.where(hit, 1.0, 0.0).astype(BF16)
    cnt[...] = jnp.broadcast_to(
        jnp.sum(jnp.where(hit, 1.0, 0.0), axis=1, keepdims=True), cnt.shape
    )
    for c in range(comp):
        xcopies[c].wait()
        for k in range(cells // 512):
            sl = pl.ds(k * 512, 512)
            sums[c, :, sl] = jnp.dot(onehot, X[c, :, sl], preferred_element_type=F32)

    def cols(q):
        return pl.ds(pl.multiple_of(q * w, w), w)

    sum_copies = []
    for d in range(1, tm):
        q = lax.rem(me_t + d, tm)
        a = pltpu.make_async_remote_copy(
            src_ref=sums.at[:, :, cols(q)], dst_ref=rsum.at[d - 1], send_sem=s_sum.at[d - 1],
            recv_sem=r_sum.at[d - 1], device_id={"tm": q}, device_id_type=MESH)
        e = pltpu.make_async_remote_copy(
            src_ref=cnt, dst_ref=rcnt.at[d - 1], send_sem=s_cnt.at[d - 1],
            recv_sem=r_cnt.at[d - 1], device_id={"tm": q}, device_id_type=MESH)
        a.start()
        e.start()
        sum_copies += [a, e]

    acc[...] = jnp.zeros_like(acc)

    def pair(p, _):
        for b in range(2):
            bb = 2 * p + b
            pltpu.make_async_copy(
                modes.at[bb], mo.at[:, pl.ds(pl.multiple_of(bb * nm, nm), nm), :], msem.at[bb]).wait()
        ms = pl.ds(pl.multiple_of(p * 2 * nm, 2 * nm), 2 * nm)

        def one(i, _):
            rs = pl.ds(pl.multiple_of(i * chunk, chunk), chunk)
            prod = lax.dot_general(X[0, rs, :], mo[0, ms, :], NT, preferred_element_type=F32)
            for c in range(1, comp):
                prod += lax.dot_general(X[c, rs, :], mo[c, ms, :], NT, preferred_element_type=F32)
            mine = binb[rs, :]
            acc[rs, :] += jnp.where(mine == 2 * p, prod[:, :nm], 0.0) + jnp.where(
                mine == 2 * p + 1, prod[:, nm:], 0.0)
            return 0

        lax.fori_loop(0, rows // chunk, one, 0)
        return 0

    half = bins // 4
    lax.fori_loop(0, half, pair, 0)

    for cp in sum_copies:
        cp.wait()
    total_cnt = cnt[...]
    for d in range(tm - 1):
        total_cnt = total_cnt + rcnt[d]
    mycols = cols(me_t)
    for c in range(comp):
        tot = sums[c, :, mycols]
        for d in range(tm - 1):
            tot = tot + rsum[d, c]
        mean[c, :, mycols] = (tot / total_cnt[:, 0:1]).astype(BF16)
    mean_copies = []
    for d in range(1, tm):
        a = pltpu.make_async_remote_copy(
            src_ref=mean.at[:, :, mycols], dst_ref=mean.at[:, :, mycols], send_sem=s_mean.at[d - 1],
            recv_sem=r_mean.at[d - 1], device_id={"tm": lax.rem(me_t + d, tm)}, device_id_type=MESH)
        a.start()
        mean_copies.append(a)

    lax.fori_loop(half, bins // 2, pair, 0)

    for d in range(1, tm):
        mean_copies[d - 1].wait_send()
        src = cols(lax.rem(me_t + tm - d, tm))
        pltpu.make_async_remote_copy(
            src_ref=mean.at[:, :, src], dst_ref=mean.at[:, :, src], send_sem=s_mean.at[d - 1],
            recv_sem=r_mean.at[d - 1], device_id={"tm": lax.rem(me_t + d, tm)}, device_id_type=MESH).wait_recv()
    mean_out[...] = mean[...]

    mj[...] = jnp.zeros_like(mj)

    def project(p, _):
        ms = pl.ds(pl.multiple_of(p * 2 * nm, 2 * nm), 2 * nm)
        prod = lax.dot_general(mean[0], mo[0, ms, :], NT, preferred_element_type=F32)
        for c in range(1, comp):
            prod += lax.dot_general(mean[c], mo[c, ms, :], NT, preferred_element_type=F32)
        own = ownb[...]
        mj[...] += jnp.where(own == 2 * p, prod[:, :nm], 0.0) + jnp.where(own == 2 * p + 1, prod[:, nm:], 0.0)
        return 0

    lax.fori_loop(0, bins // 2, project, 0)

    def block(s):
        return pl.ds(pl.multiple_of(s * blk, blk), blk)

    def corrected(s):
        rs = block(s)
        v = acc[rs, :]
        mine = binb[rs, :]
        for j in range(bins):
            v = v - jnp.where(mine == ownb[j:j + 1, :], mj[j:j + 1, :], 0.0)
        return v

    rs_copies = []
    for d in range(1, space):
        q = lax.rem(me_s + d, space)
        sendc[d - 1] = corrected(q).astype(BF16)
        a = pltpu.make_async_remote_copy(
            src_ref=sendc.at[d - 1], dst_ref=rsc.at[d - 1], send_sem=s_rs.at[d - 1],
            recv_sem=r_rs.at[d - 1], device_id={"space": q}, device_id_type=MESH)
        a.start()
        rs_copies.append(a)
    tot = corrected(me_s)
    for d in range(space - 1):
        rs_copies[d].wait()
        tot = tot + rsc[d].astype(F32)
    mine = block(me_s)
    agc[mine, :] = tot.astype(BF16)
    ag_copies = []
    for d in range(1, space):
        a = pltpu.make_async_remote_copy(
            src_ref=agc.at[mine], dst_ref=agc.at[mine], send_sem=s_ag.at[d - 1],
            recv_sem=r_ag.at[d - 1], device_id={"space": lax.rem(me_s + d, space)}, device_id_type=MESH)
        a.start()
        ag_copies.append(a)
    for d in range(1, space):
        ag_copies[d - 1].wait_send()
        src = block(lax.rem(me_s + space - d, space))
        pltpu.make_async_remote_copy(
            src_ref=agc.at[src], dst_ref=agc.at[src], send_sem=s_ag.at[d - 1],
            recv_sem=r_ag.at[d - 1], device_id={"space": lax.rem(me_s + d, space)}, device_id_type=MESH).wait_recv()
    coef_out[...] = agc[...]


def on_device(snaps, phase_bin, owner_order, modes):
    rows, comp, cells = snaps.shape
    bins, nm = modes.shape[0], modes.shape[1]
    tm, space = lax.axis_size("tm"), lax.axis_size("space")
    blk, w = rows // space, cells // tm
    binrow = phase_bin.reshape(1, rows)
    binb = jnp.broadcast_to(phase_bin[:, None], (rows, nm))
    ownb = jnp.broadcast_to(owner_order[:, None], (bins, nm))
    vm = pl.BlockSpec(memory_space=pltpu.VMEM)
    hbm = pl.BlockSpec(memory_space=pl.ANY)
    dma = pltpu.SemaphoreType.DMA
    coef, mean = pl.pallas_call(
        functools.partial(kernel, tm, space),
        out_shape=(
            jax.ShapeDtypeStruct((rows, nm), BF16),
            jax.ShapeDtypeStruct((comp, bins, cells), BF16),
        ),
        in_specs=[vm, vm, vm, hbm, hbm],
        out_specs=(vm, vm),
        scratch_shapes=[
            pltpu.VMEM((comp, rows, cells), BF16),
            pltpu.VMEM((comp, bins * nm, cells), BF16),
            pltpu.VMEM((rows, nm), F32),
            pltpu.VMEM((comp, bins, cells), F32),
            pltpu.VMEM((bins, 128), F32),
            pltpu.VMEM((tm - 1, comp, bins, w), F32),
            pltpu.VMEM((tm - 1, bins, 128), F32),
            pltpu.VMEM((comp, bins, cells), BF16),
            pltpu.VMEM((space - 1, blk, nm), BF16),
            pltpu.VMEM((space - 1, blk, nm), BF16),
            pltpu.VMEM((rows, nm), BF16),
            pltpu.VMEM((bins, nm), F32),
            dma((comp,)), dma((bins,)),
            dma((tm - 1,)), dma((tm - 1,)), dma((tm - 1,)), dma((tm - 1,)), dma((tm - 1,)), dma((tm - 1,)),
            dma((space - 1,)), dma((space - 1,)), dma((space - 1,)), dma((space - 1,)),
        ],
        compiler_params=pltpu.CompilerParams(
            collective_id=0, has_side_effects=True, vmem_limit_bytes=56 * 1024 * 1024
        ),
        cost_estimate=pl.CostEstimate(
            flops=2 * rows * bins * nm * comp * cells,
            bytes_accessed=2 * comp * cells * (rows + bins * nm), transcendentals=0),
    )(binrow, binb, ownb, snaps.transpose(1, 0, 2), modes.transpose(0, 2, 1, 3))
    own_rows = bins // tm
    own = lax.dynamic_slice_in_dim(mean, lax.axis_index("tm") * own_rows, own_rows, 1)
    return own.transpose(1, 0, 2), coef.astype(F32)


def solution(mesh):
    in_specs = (P("tm", None, "space"), P("tm"), P(), P(None, None, None, "space"))
    out_specs = (P("tm", None, "space"), P("tm", None))
    return jax.shard_map(
        on_device, mesh=mesh, in_specs=in_specs, out_specs=out_specs, check_vma=False
    )
```

```python
import functools

import jax
import jax.numpy as jnp
from jax import lax
from jax.experimental import pallas as pl
from jax.experimental.pallas import tpu as pltpu
from jax.sharding import PartitionSpec as P

MESH = pl.DeviceIdType.MESH
F32 = jnp.float32
BF16 = jnp.bfloat16
NT = (((1,), (1,)), ((), ()))


def kernel(
    tm, space, binrow, ownrow, snaps, modes, coef_out, mean_out,
    binb, ownb, X, mo, acc, sums, cnt, rsum, rcnt, mean, sendc, rsc, agc, mj,
    xsem, msem, s_sum, r_sum, s_cnt, r_cnt, s_mean, r_mean, s_rs, r_rs, s_ag, r_ag,
):
    comp, rows, cells = X.shape
    bins = modes.shape[0]
    nm = modes.shape[2]
    w = cells // tm
    blk = rows // space
    chunk = 1024
    me_t = lax.axis_index("tm")
    me_s = lax.axis_index("space")

    xcopies = [pltpu.make_async_copy(snaps.at[c], X.at[c], xsem.at[c]) for c in range(comp)]
    for cp in xcopies:
        cp.start()

    barrier = pltpu.get_barrier_semaphore()
    for d in range(1, tm):
        pl.semaphore_signal(barrier, inc=1, device_id={"tm": lax.rem(me_t + d, tm)}, device_id_type=MESH)
    for d in range(1, space):
        pl.semaphore_signal(barrier, inc=1, device_id={"space": lax.rem(me_s + d, space)}, device_id_type=MESH)
    pl.semaphore_wait(barrier, tm - 1 + space - 1)

    for k in range(rows // nm):
        sl = pl.ds(k * nm, nm)
        binb[sl, :] = jnp.broadcast_to(binrow[:, sl], (nm, nm)).T
    diagonal = lax.broadcasted_iota(jnp.int32, (bins, bins), 0) == lax.broadcasted_iota(
        jnp.int32, (bins, bins), 1)
    picked = jnp.where(diagonal, jnp.broadcast_to(ownrow[...].astype(F32), (bins, bins)), 0.0)
    ownb[...] = jnp.broadcast_to(
        jnp.sum(picked, axis=1, keepdims=True).astype(jnp.int32), ownb.shape)

    fetch = [[], [0, 1], list(range(2, bins))]

    hit = ownb[:, 0:1] == binrow[...]
    onehot = jnp.where(hit, 1.0, 0.0).astype(BF16)
    cnt[...] = jnp.broadcast_to(
        jnp.sum(jnp.where(hit, 1.0, 0.0), axis=1, keepdims=True), cnt.shape
    )
    for c in range(comp):
        xcopies[c].wait()
        for b in fetch[c]:
            pltpu.make_async_copy(modes.at[b], mo.at[:, pl.ds(b * nm, nm), :], msem.at[b]).start()
        for k in range(cells // 512):
            sl = pl.ds(k * 512, 512)
            sums[c, :, sl] = jnp.dot(onehot, X[c, :, sl], preferred_element_type=F32)

    def cols(q):
        return pl.ds(pl.multiple_of(q * w, w), w)

    sum_copies = []
    for d in range(1, tm):
        q = lax.rem(me_t + d, tm)
        a = pltpu.make_async_remote_copy(
            src_ref=sums.at[:, :, cols(q)], dst_ref=rsum.at[d - 1], send_sem=s_sum.at[d - 1],
            recv_sem=r_sum.at[d - 1], device_id={"tm": q}, device_id_type=MESH)
        e = pltpu.make_async_remote_copy(
            src_ref=cnt, dst_ref=rcnt.at[d - 1], send_sem=s_cnt.at[d - 1],
            recv_sem=r_cnt.at[d - 1], device_id={"tm": q}, device_id_type=MESH)
        a.start()
        e.start()
        sum_copies += [a, e]

    acc[...] = jnp.zeros_like(acc)

    def pair(p, _):
        for b in range(2):
            bb = 2 * p + b
            pltpu.make_async_copy(
                modes.at[bb], mo.at[:, pl.ds(pl.multiple_of(bb * nm, nm), nm), :], msem.at[bb]).wait()
        ms = pl.ds(pl.multiple_of(p * 2 * nm, 2 * nm), 2 * nm)

        def one(i, _):
            rs = pl.ds(pl.multiple_of(i * chunk, chunk), chunk)
            prod = lax.dot_general(X[0, rs, :], mo[0, ms, :], NT, preferred_element_type=F32)
            for c in range(1, comp):
                prod += lax.dot_general(X[c, rs, :], mo[c, ms, :], NT, preferred_element_type=F32)
            mine = binb[rs, :]
            acc[rs, :] += jnp.where(mine == 2 * p, prod[:, :nm], 0.0) + jnp.where(
                mine == 2 * p + 1, prod[:, nm:], 0.0)
            return 0

        lax.fori_loop(0, rows // chunk, one, 0)
        return 0

    half = bins // 4
    lax.fori_loop(0, half, pair, 0)

    for cp in sum_copies:
        cp.wait()
    total_cnt = cnt[...]
    for d in range(tm - 1):
        total_cnt = total_cnt + rcnt[d]
    mycols = cols(me_t)
    for c in range(comp):
        tot = sums[c, :, mycols]
        for d in range(tm - 1):
            tot = tot + rsum[d, c]
        mean[c, :, mycols] = (tot / total_cnt[:, 0:1]).astype(BF16)
    mean_copies = []
    for d in range(1, tm):
        a = pltpu.make_async_remote_copy(
            src_ref=mean.at[:, :, mycols], dst_ref=mean.at[:, :, mycols], send_sem=s_mean.at[d - 1],
            recv_sem=r_mean.at[d - 1], device_id={"tm": lax.rem(me_t + d, tm)}, device_id_type=MESH)
        a.start()
        mean_copies.append(a)

    lax.fori_loop(half, bins // 2, pair, 0)

    for d in range(1, tm):
        mean_copies[d - 1].wait_send()
        src = cols(lax.rem(me_t + tm - d, tm))
        pltpu.make_async_remote_copy(
            src_ref=mean.at[:, :, src], dst_ref=mean.at[:, :, src], send_sem=s_mean.at[d - 1],
            recv_sem=r_mean.at[d - 1], device_id={"tm": lax.rem(me_t + d, tm)}, device_id_type=MESH).wait_recv()
    mean_out[...] = mean[...]

    mj[...] = jnp.zeros_like(mj)

    def project(p, _):
        ms = pl.ds(pl.multiple_of(p * 2 * nm, 2 * nm), 2 * nm)
        prod = lax.dot_general(mean[0], mo[0, ms, :], NT, preferred_element_type=F32)
        for c in range(1, comp):
            prod += lax.dot_general(mean[c], mo[c, ms, :], NT, preferred_element_type=F32)
        own = ownb[...]
        mj[...] += jnp.where(own == 2 * p, prod[:, :nm], 0.0) + jnp.where(own == 2 * p + 1, prod[:, nm:], 0.0)
        return 0

    lax.fori_loop(0, bins // 2, project, 0)

    def block(s):
        return pl.ds(pl.multiple_of(s * blk, blk), blk)

    def corrected(s):
        rs = block(s)
        v = acc[rs, :]
        mine = binb[rs, :]
        for j in range(bins):
            v = v - jnp.where(mine == ownb[j:j + 1, :], mj[j:j + 1, :], 0.0)
        return v

    rs_copies = []
    for d in range(1, space):
        q = lax.rem(me_s + d, space)
        sendc[d - 1] = corrected(q).astype(BF16)
        a = pltpu.make_async_remote_copy(
            src_ref=sendc.at[d - 1], dst_ref=rsc.at[d - 1], send_sem=s_rs.at[d - 1],
            recv_sem=r_rs.at[d - 1], device_id={"space": q}, device_id_type=MESH)
        a.start()
        rs_copies.append(a)
    tot = corrected(me_s)
    for d in range(space - 1):
        rs_copies[d].wait()
        tot = tot + rsc[d].astype(F32)
    mine = block(me_s)
    agc[mine, :] = tot.astype(BF16)
    ag_copies = []
    for d in range(1, space):
        a = pltpu.make_async_remote_copy(
            src_ref=agc.at[mine], dst_ref=agc.at[mine], send_sem=s_ag.at[d - 1],
            recv_sem=r_ag.at[d - 1], device_id={"space": lax.rem(me_s + d, space)}, device_id_type=MESH)
        a.start()
        ag_copies.append(a)
    for d in range(1, space):
        ag_copies[d - 1].wait_send()
        src = block(lax.rem(me_s + space - d, space))
        pltpu.make_async_remote_copy(
            src_ref=agc.at[src], dst_ref=agc.at[src], send_sem=s_ag.at[d - 1],
            recv_sem=r_ag.at[d - 1], device_id={"space": lax.rem(me_s + d, space)}, device_id_type=MESH).wait_recv()
    coef_out[...] = agc[...]


def on_device(snaps, phase_bin, owner_order, modes):
    rows, comp, cells = snaps.shape
    bins, nm = modes.shape[0], modes.shape[1]
    tm, space = lax.axis_size("tm"), lax.axis_size("space")
    blk, w = rows // space, cells // tm
    binrow = phase_bin.reshape(1, rows)
    ownrow = owner_order.reshape(1, bins)
    vm = pl.BlockSpec(memory_space=pltpu.VMEM)
    hbm = pl.BlockSpec(memory_space=pl.ANY)
    dma = pltpu.SemaphoreType.DMA
    coef, mean = pl.pallas_call(
        functools.partial(kernel, tm, space),
        out_shape=(
            jax.ShapeDtypeStruct((rows, nm), BF16),
            jax.ShapeDtypeStruct((comp, bins, cells), BF16),
        ),
        in_specs=[vm, vm, hbm, hbm],
        out_specs=(vm, vm),
        scratch_shapes=[
            pltpu.VMEM((rows, nm), jnp.int32),
            pltpu.VMEM((bins, nm), jnp.int32),
            pltpu.VMEM((comp, rows, cells), BF16),
            pltpu.VMEM((comp, bins * nm, cells), BF16),
            pltpu.VMEM((rows, nm), F32),
            pltpu.VMEM((comp, bins, cells), F32),
            pltpu.VMEM((bins, 128), F32),
            pltpu.VMEM((tm - 1, comp, bins, w), F32),
            pltpu.VMEM((tm - 1, bins, 128), F32),
            pltpu.VMEM((comp, bins, cells), BF16),
            pltpu.VMEM((space - 1, blk, nm), BF16),
            pltpu.VMEM((space - 1, blk, nm), BF16),
            pltpu.VMEM((rows, nm), BF16),
            pltpu.VMEM((bins, nm), F32),
            dma((comp,)), dma((bins,)),
            dma((tm - 1,)), dma((tm - 1,)), dma((tm - 1,)), dma((tm - 1,)), dma((tm - 1,)), dma((tm - 1,)),
            dma((space - 1,)), dma((space - 1,)), dma((space - 1,)), dma((space - 1,)),
        ],
        compiler_params=pltpu.CompilerParams(
            collective_id=0, has_side_effects=True, vmem_limit_bytes=56 * 1024 * 1024
        ),
        cost_estimate=pl.CostEstimate(
            flops=2 * rows * bins * nm * comp * cells,
            bytes_accessed=2 * comp * cells * (rows + bins * nm), transcendentals=0),
    )(binrow, ownrow, snaps.transpose(1, 0, 2), modes.transpose(0, 2, 1, 3))
    own_rows = bins // tm
    own = lax.dynamic_slice_in_dim(mean, lax.axis_index("tm") * own_rows, own_rows, 1)
    return own.transpose(1, 0, 2), coef.astype(F32)


def solution(mesh):
    in_specs = (P("tm", None, "space"), P("tm"), P(), P(None, None, None, "space"))
    out_specs = (P("tm", None, "space"), P("tm", None))
    return jax.shard_map(
        on_device, mesh=mesh, in_specs=in_specs, out_specs=out_specs, check_vma=False
    )
```

```python
import functools

import jax
import jax.numpy as jnp
from jax import lax
from jax.experimental import pallas as pl
from jax.experimental.pallas import tpu as pltpu
from jax.sharding import PartitionSpec as P

MESH = pl.DeviceIdType.MESH
F32 = jnp.float32
BF16 = jnp.bfloat16
NT = (((1,), (1,)), ((), ()))


def kernel(
    tm, space, binrow, ownrow, snaps, modes, coef_out, mean_out,
    binb, ownb, X, mo, acc, sums, cnt, rsum, rcnt, sendc, rsc, agc, mj,
    xsem, msem, s_sum, r_sum, s_cnt, r_cnt, s_mean, r_mean, s_rs, r_rs, s_ag, r_ag,
):
    comp, rows, cells = snaps.shape
    bins = modes.shape[0]
    nm = modes.shape[2]
    w = cells // tm
    blk = rows // space
    chunk = rows
    me_t = lax.axis_index("tm")
    me_s = lax.axis_index("space")

    xcopies = [pltpu.make_async_copy(snaps.at[c], X.at[c, pl.ds(0, rows), :], xsem.at[c]) for c in range(comp)]
    for cp in xcopies:
        cp.start()

    barrier = pltpu.get_barrier_semaphore()
    for d in range(1, tm):
        pl.semaphore_signal(barrier, inc=1, device_id={"tm": lax.rem(me_t + d, tm)}, device_id_type=MESH)
    for d in range(1, space):
        pl.semaphore_signal(barrier, inc=1, device_id={"space": lax.rem(me_s + d, space)}, device_id_type=MESH)
    pl.semaphore_wait(barrier, tm - 1 + space - 1)

    for k in range(rows // nm):
        sl = pl.ds(k * nm, nm)
        binb[sl, :] = jnp.broadcast_to(binrow[:, sl], (nm, nm)).T
    diagonal = lax.broadcasted_iota(jnp.int32, (bins, bins), 0) == lax.broadcasted_iota(
        jnp.int32, (bins, bins), 1)
    picked = jnp.where(diagonal, jnp.broadcast_to(ownrow[...].astype(F32), (bins, bins)), 0.0)
    ownb[...] = jnp.broadcast_to(
        jnp.sum(picked, axis=1, keepdims=True).astype(jnp.int32), ownb.shape)

    fetch = [[], [0, 1], list(range(2, bins))]

    hit = ownb[:, 0:1] == binrow[...]
    onehot = jnp.where(hit, 1.0, 0.0).astype(BF16)
    cnt[...] = jnp.broadcast_to(
        jnp.sum(jnp.where(hit, 1.0, 0.0), axis=1, keepdims=True), cnt.shape
    )
    for c in range(comp):
        xcopies[c].wait()
        for b in fetch[c]:
            pltpu.make_async_copy(modes.at[b], mo.at[:, pl.ds(b * nm, nm), :], msem.at[b]).start()
        for k in range(cells // 512):
            sl = pl.ds(k * 512, 512)
            sums[c, :, sl] = jnp.dot(onehot, X[c, :rows, sl], preferred_element_type=F32)

    def cols(q):
        return pl.ds(pl.multiple_of(q * w, w), w)

    sum_copies = []
    for d in range(1, tm):
        q = lax.rem(me_t + d, tm)
        a = pltpu.make_async_remote_copy(
            src_ref=sums.at[:, :, cols(q)], dst_ref=rsum.at[d - 1], send_sem=s_sum.at[d - 1],
            recv_sem=r_sum.at[d - 1], device_id={"tm": q}, device_id_type=MESH)
        e = pltpu.make_async_remote_copy(
            src_ref=cnt, dst_ref=rcnt.at[d - 1], send_sem=s_cnt.at[d - 1],
            recv_sem=r_cnt.at[d - 1], device_id={"tm": q}, device_id_type=MESH)
        a.start()
        e.start()
        sum_copies += [a, e]

    acc[...] = jnp.zeros_like(acc)

    def pair(p, _):
        for b in range(2):
            bb = 2 * p + b
            pltpu.make_async_copy(
                modes.at[bb], mo.at[:, pl.ds(pl.multiple_of(bb * nm, nm), nm), :], msem.at[bb]).wait()
        ms = pl.ds(pl.multiple_of(p * 2 * nm, 2 * nm), 2 * nm)

        def one(i, _):
            rs = pl.ds(pl.multiple_of(i * chunk, chunk), chunk)
            prod = lax.dot_general(X[0, rs, :], mo[0, ms, :], NT, preferred_element_type=F32)
            for c in range(1, comp):
                prod += lax.dot_general(X[c, rs, :], mo[c, ms, :], NT, preferred_element_type=F32)
            mine = binb[rs, :]
            acc[rs, :] += jnp.where(mine == 2 * p, prod[:, :nm], 0.0) + jnp.where(
                mine == 2 * p + 1, prod[:, nm:], 0.0)
            return 0

        lax.fori_loop(0, rows // chunk, one, 0)
        return 0

    half = bins // 4
    lax.fori_loop(0, half, pair, 0)

    for cp in sum_copies:
        cp.wait()
    total_cnt = cnt[...]
    for d in range(tm - 1):
        total_cnt = total_cnt + rcnt[d]
    mycols = cols(me_t)
    for c in range(comp):
        tot = sums[c, :, mycols]
        for d in range(tm - 1):
            tot = tot + rsum[d, c]
        X[c, rows:, mycols] = (tot / total_cnt[:, 0:1]).astype(BF16)
    mean_copies = []
    for d in range(1, tm):
        a = pltpu.make_async_remote_copy(
            src_ref=X.at[:, pl.ds(rows, bins), mycols], dst_ref=X.at[:, pl.ds(rows, bins), mycols], send_sem=s_mean.at[d - 1],
            recv_sem=r_mean.at[d - 1], device_id={"tm": lax.rem(me_t + d, tm)}, device_id_type=MESH)
        a.start()
        mean_copies.append(a)

    late = bins // 2 - 2
    lax.fori_loop(half, late, pair, 0)

    for d in range(1, tm):
        mean_copies[d - 1].wait_send()
        src = cols(lax.rem(me_t + tm - d, tm))
        pltpu.make_async_remote_copy(
            src_ref=X.at[:, pl.ds(rows, bins), src], dst_ref=X.at[:, pl.ds(rows, bins), src], send_sem=s_mean.at[d - 1],
            recv_sem=r_mean.at[d - 1], device_id={"tm": lax.rem(me_t + d, tm)}, device_id_type=MESH).wait_recv()
    mean_out[...] = X[:, rows:, :]

    mj[...] = jnp.zeros_like(mj)

    def project(p, _):
        ms = pl.ds(pl.multiple_of(p * 2 * nm, 2 * nm), 2 * nm)
        prod = lax.dot_general(X[0, rows:, :], mo[0, ms, :], NT, preferred_element_type=F32)
        for c in range(1, comp):
            prod += lax.dot_general(X[c, rows:, :], mo[c, ms, :], NT, preferred_element_type=F32)
        own = ownb[...]
        mj[...] += jnp.where(own == 2 * p, prod[:, :nm], 0.0) + jnp.where(own == 2 * p + 1, prod[:, nm:], 0.0)
        return 0

    def pair_and_mean(p, _):
        for b in range(2):
            bb = 2 * p + b
            pltpu.make_async_copy(
                modes.at[bb], mo.at[:, pl.ds(pl.multiple_of(bb * nm, nm), nm), :], msem.at[bb]).wait()
        ms = pl.ds(pl.multiple_of(p * 2 * nm, 2 * nm), 2 * nm)
        prod = lax.dot_general(X[0], mo[0, ms, :], NT, preferred_element_type=F32)
        for c in range(1, comp):
            prod += lax.dot_general(X[c], mo[c, ms, :], NT, preferred_element_type=F32)
        for which, part, into in ((binb, prod[:rows], acc), (ownb, prod[rows:], mj)):
            into[...] += jnp.where(which[...] == 2 * p, part[:, :nm], 0.0) + jnp.where(
                which[...] == 2 * p + 1, part[:, nm:], 0.0)
        return 0

    lax.fori_loop(late, bins // 2, pair_and_mean, 0)
    lax.fori_loop(0, late, project, 0)

    def block(s):
        return pl.ds(pl.multiple_of(s * blk, blk), blk)

    def corrected(s):
        rs = block(s)
        v = acc[rs, :]
        mine = binb[rs, :]
        for j in range(bins):
            v = v - jnp.where(mine == ownb[j:j + 1, :], mj[j:j + 1, :], 0.0)
        return v

    rs_copies = []
    for d in range(1, space):
        q = lax.rem(me_s + d, space)
        sendc[d - 1] = corrected(q).astype(BF16)
        a = pltpu.make_async_remote_copy(
            src_ref=sendc.at[d - 1], dst_ref=rsc.at[d - 1], send_sem=s_rs.at[d - 1],
            recv_sem=r_rs.at[d - 1], device_id={"space": q}, device_id_type=MESH)
        a.start()
        rs_copies.append(a)
    tot = corrected(me_s)
    for d in range(space - 1):
        rs_copies[d].wait()
        tot = tot + rsc[d].astype(F32)
    mine = block(me_s)
    agc[mine, :] = tot.astype(BF16)
    ag_copies = []
    for d in range(1, space):
        a = pltpu.make_async_remote_copy(
            src_ref=agc.at[mine], dst_ref=agc.at[mine], send_sem=s_ag.at[d - 1],
            recv_sem=r_ag.at[d - 1], device_id={"space": lax.rem(me_s + d, space)}, device_id_type=MESH)
        a.start()
        ag_copies.append(a)
    for d in range(1, space):
        ag_copies[d - 1].wait_send()
        src = block(lax.rem(me_s + space - d, space))
        pltpu.make_async_remote_copy(
            src_ref=agc.at[src], dst_ref=agc.at[src], send_sem=s_ag.at[d - 1],
            recv_sem=r_ag.at[d - 1], device_id={"space": lax.rem(me_s + d, space)}, device_id_type=MESH).wait_recv()
    coef_out[...] = agc[...]


def on_device(snaps, phase_bin, owner_order, modes):
    rows, comp, cells = snaps.shape
    bins, nm = modes.shape[0], modes.shape[1]
    tm, space = lax.axis_size("tm"), lax.axis_size("space")
    blk, w = rows // space, cells // tm
    binrow = phase_bin.reshape(1, rows)
    ownrow = owner_order.reshape(1, bins)
    vm = pl.BlockSpec(memory_space=pltpu.VMEM)
    hbm = pl.BlockSpec(memory_space=pl.ANY)
    dma = pltpu.SemaphoreType.DMA
    coef, mean = pl.pallas_call(
        functools.partial(kernel, tm, space),
        out_shape=(
            jax.ShapeDtypeStruct((rows, nm), BF16),
            jax.ShapeDtypeStruct((comp, bins, cells), BF16),
        ),
        in_specs=[vm, vm, hbm, hbm],
        out_specs=(vm, vm),
        scratch_shapes=[
            pltpu.VMEM((rows, nm), jnp.int32),
            pltpu.VMEM((bins, nm), jnp.int32),
            pltpu.VMEM((comp, rows + bins, cells), BF16),
            pltpu.VMEM((comp, bins * nm, cells), BF16),
            pltpu.VMEM((rows, nm), F32),
            pltpu.VMEM((comp, bins, cells), F32),
            pltpu.VMEM((bins, 128), F32),
            pltpu.VMEM((tm - 1, comp, bins, w), F32),
            pltpu.VMEM((tm - 1, bins, 128), F32),
            pltpu.VMEM((space - 1, blk, nm), BF16),
            pltpu.VMEM((space - 1, blk, nm), BF16),
            pltpu.VMEM((rows, nm), BF16),
            pltpu.VMEM((bins, nm), F32),
            dma((comp,)), dma((bins,)),
            dma((tm - 1,)), dma((tm - 1,)), dma((tm - 1,)), dma((tm - 1,)), dma((tm - 1,)), dma((tm - 1,)),
            dma((space - 1,)), dma((space - 1,)), dma((space - 1,)), dma((space - 1,)),
        ],
        compiler_params=pltpu.CompilerParams(
            collective_id=0, has_side_effects=True, vmem_limit_bytes=56 * 1024 * 1024
        ),
        cost_estimate=pl.CostEstimate(
            flops=2 * rows * bins * nm * comp * cells,
            bytes_accessed=2 * comp * cells * (rows + bins * nm), transcendentals=0),
    )(binrow, ownrow, snaps.transpose(1, 0, 2), modes.transpose(0, 2, 1, 3))
    own_rows = bins // tm
    own = lax.dynamic_slice_in_dim(mean, lax.axis_index("tm") * own_rows, own_rows, 1)
    return own.transpose(1, 0, 2), coef.astype(F32)


def solution(mesh):
    in_specs = (P("tm", None, "space"), P("tm"), P(), P(None, None, None, "space"))
    out_specs = (P("tm", None, "space"), P("tm", None))
    return jax.shard_map(
        on_device, mesh=mesh, in_specs=in_specs, out_specs=out_specs, check_vma=False
    )
```
